512 devices in a mesh: gx: 8 (over z_lo), gy: 8 (over y, z_hi), gz: 8 (over x, core).
Axes of the slice: x: 4, y: 4, z: 16 (z_hi: 2, z_lo: 8; z = z_hi * 8 + z_lo), core: 2. Of those that a mesh axis runs over, the one named last changes fastest.
Arguments:
- hidden_pre: bfloat16 [2048, 24576], P('gy', ('gz', 'gx')), may hold values from -6 to 6
- grad_out: bfloat16 [2048, 12288], P(('gx', 'gz'), 'gy'), may hold values from -16 to 16
- down_weight: bfloat16 [24576, 12288], P(('gz', 'gx'), 'gy'), may hold values from -0.0546875 to 0.0546875
Outputs:
- grad_hidden: bfloat16 [2048, 24576], P('gy', ('gz', 'gx'))
- grad_weight: float32 [24576, 12288], P(('gz', 'gx'), 'gy')
The draws below stay inside these ranges and needn't reach their ends.
All inputs are finite; a program needn't handle non-finite values.
Results may differ from the reference program's by a relative error of at most 0.0029.
Values may be sent and summed in bfloat16 or wider, within the bound.
A program may use at most 64 MiB of HBM per device.

```python
import math
import jax
import jax.numpy as jnp
from jax import lax

D = 12288
HIDDEN_SIZE = 24576
TOKENS = 2048


def raised(array, key, source, target, blocks, factor):
    owner, partner = [(jnp.arange(array.shape[axis_at]) // (array.shape[axis_at] // blocks)).reshape([-1 if axis == axis_at else 1 for axis in range(array.ndim)]) for axis_at in (source, target)]
    chosen = jax.random.permutation(key, blocks)[partner]
    strong = (owner == chosen) | (owner == (partner + blocks // 2) % blocks)
    return jnp.where(strong, factor * array, array)


def levels(key, shape, pieces, low, top_value):
    factor_of = 1.0
    for axis_at, blocks in pieces:
        steps = jax.random.uniform(jax.random.fold_in(jax.random.fold_in(key, 6), axis_at), (blocks,), jnp.float32, low / len(pieces), top_value / len(pieces))
        factor_of = factor_of * jnp.repeat(jnp.exp(steps), shape[axis_at] // blocks).reshape((-1,) + (1,) * (len(shape) - 1 - axis_at))
    return factor_of


def gaussian(stream_key, dims, width, reach, shards=(), dtype=jnp.bfloat16):
    gain = levels(stream_key, dims, shards, -0.22, 0.18) if shards else 1.0
    result = jax.random.normal(stream_key, dims, jnp.float32) * width * gain
    return jnp.minimum(jnp.maximum(result, -reach), reach).astype(dtype)


def heavy_noise(key, dims, width, reach, pieces, heavy, held_as=jnp.bfloat16):
    result = width * jax.random.normal(key, dims, jnp.float32)
    if pieces:
        result = result * levels(key, dims, pieces, -0.22, 0.18)
    return jnp.clip(raised(result, jax.random.fold_in(key, 3), *heavy), -reach, reach).astype(held_as)


def setup_inputs(seed: int = 0) -> dict:
    key_list = jax.random.split(jax.random.key(seed), 4)
    return {
        "hidden_pre": gaussian(key_list[0], (TOKENS, HIDDEN_SIZE), 1.0, 6.0, ((0, 8), (1, 64))),
        "grad_out": heavy_noise(key_list[1], (TOKENS, D), 1.0, 16.0, ((0, 64), (1, 8)), (1, 0, 64, 4.0)),
        "down_weight": gaussian(key_list[2], (HIDDEN_SIZE, D), D ** -0.5, 0.0546875, ((0, 64), (1, 8))),
    }


coeff = math.sqrt(2.0 / math.pi)

def gelu_value(h):
    inner = coeff * (h + 0.044715 * h * h * h)
    return 0.5 * h * (1.0 + jnp.tanh(inner))

def gelu_slope(h):
    inner = coeff * (h + 0.044715 * h * h * h)
    tval = jnp.tanh(inner)
    return 0.5 * (1.0 + tval) + 0.5 * h * (1.0 - tval * tval) * coeff * (1.0 + 3.0 * 0.044715 * h * h)

def reference(hidden_pre, grad_out, down_weight):
    hfull = hidden_pre.astype(jnp.float32)
    act = gelu_value(hfull).astype(jnp.bfloat16)
    grad_weight = lax.dot_general(act, grad_out, (((0,), (0,)), ((), ())), preferred_element_type=jnp.float32)
    grad_act = lax.dot_general(grad_out, down_weight, (((1,), (1,)), ((), ())), preferred_element_type=jnp.float32)
    grad_hidden = (grad_act * gelu_slope(hfull)).astype(jnp.bfloat16)
    return (grad_hidden, grad_weight)
```

```python
import math

import jax
import jax.numpy as jnp
from jax import lax
from jax.experimental import pallas as pl
from jax.experimental.pallas import tpu as pltpu
from jax.sharding import PartitionSpec as P

MESH = pl.DeviceIdType.MESH
coeff = math.sqrt(2.0 / math.pi)

NZ, NY, NX = 8, 4, 4
BLK = 32
TOK = 256
QTR = TOK // NY
FEAT = 1536
HID = 384
TILE = 256
NT = FEAT // TILE
ACT_SEND, ACT_PASS = 3, 10
LAST = 13


def kernel(h_ref, g_ref, w_hbm, gh_ref, dw_hbm,
           rows_all, w_ref, act_t, slope, part, from_y, kept, z_out, z_in, full, dw_buf,
           w_sem, dw_sem, zs, zr, xs, xr, hs, hr, cs, cr, ys, yr, ts, tr, as_, ar, fs, fr):
    gx, gy, gz = lax.axis_index("gx"), lax.axis_index("gy"), lax.axis_index("gz")
    y, zh = gy // 2, gy % 2
    x, c = gz // 2, gz % 2
    z = gx

    def at_z(v):
        return {"gx": v, "gy": gy, "gz": gz}

    def at_x(o):
        return {"gx": gx, "gy": gy, "gz": ((x + o) % NX) * 2 + c}

    def at_y(v):
        return {"gx": gx, "gy": v * 2 + zh, "gz": gz}

    twin = {"gx": gx, "gy": gy, "gz": x * 2 + (1 - c)}
    far = {"gx": gx, "gy": y * 2 + (1 - zh), "gz": gz}

    def block(j, xx, cc, start=0, size=BLK):
        return rows_all.at[pl.ds(pl.multiple_of(((j * NX + xx) * 2 + cc) * BLK + start, 16), size)]

    def remote(src, dst, send, recv, to):
        return pltpu.make_async_remote_copy(
            src_ref=src, dst_ref=dst, send_sem=send, recv_sem=recv, device_id=to, device_id_type=MESH)

    def z_copy(j, up):
        b = block(j, x, c)
        return remote(b, b, zs.at[up, j], zr.at[j], at_z(z + 1 if up else z - 1))

    def x_copy(j, up):
        b = block(j, x, c)
        return remote(b, b, xs.at[up, j], xr.at[up, j], at_x(1 if up else -1))

    def x_came(j, up):
        b = block(j, (x + (NX - 1 if up else 1)) % NX, c)
        return remote(b, b, xs.at[up, j], xr.at[up, j], at_x(1 if up else -1))

    def half_copy(j, up):
        b = block(j, (x + (NX - 1 if up else 1)) % NX, c, 0 if up else 16, 16)
        return remote(b, b, hs.at[up, j], hr.at[up, j], at_x(1 if up else -1))

    def half_came(j, up):
        b = block(j, (x + 2) % NX, c, 0 if up else 16, 16)
        return remote(b, b, hs.at[up, j], hr.at[up, j], at_x(1 if up else -1))

    def c_copy(j, o):
        b = block(j, (x + o) % NX, c)
        return remote(b, b, cs.at[o, j], cr.at[o, j], twin)

    def c_came(j, o):
        b = block(j, (x + o) % NX, 1 - c)
        return remote(b, b, cs.at[o, j], cr.at[o, j], twin)

    def y_copy(j, o):
        yt = (y + o) % NY
        return remote(part.at[j, pl.ds(pl.multiple_of(yt * QTR, QTR), QTR)], from_y.at[o - 1, j],
                      ys.at[o - 1, j], yr.at[o - 1, j], at_y(yt))

    def far_copy(k):
        return remote(z_out.at[k], z_in.at[k], ts.at[k], tr.at[k], far)

    def full_copy(k):
        return remote(kept.at[k], full.at[pl.ds(pl.multiple_of(y * QTR, QTR), QTR)], fs.at[k], fr.at[y], at_y(k))

    def full_came(o):
        yt = (y + o) % NY
        return remote(kept.at[yt], full.at[pl.ds(pl.multiple_of(yt * QTR, QTR), QTR)], fs.at[yt], fr.at[yt], at_y(yt))

    def act_block(g):
        return act_t.at[:, pl.ds(pl.multiple_of(g * TOK, TOK), TOK)]

    def act_far():
        return remote(act_block(gy), act_block(gy), as_.at[0], ar.at[gy], far)

    def act_far_came():
        b = act_block(y * 2 + 1 - zh)
        return remote(b, b, as_.at[0], ar.at[y * 2 + 1 - zh], far)

    def act_copy(own, o):
        g = gy if own else y * 2 + 1 - zh
        return remote(act_block(g), act_block(g), as_.at[o + (0 if own else 3)], ar.at[g], at_y((y + o) % NY))

    def act_came(own, o):
        g = ((y + o) % NY) * 2 + (zh if own else 1 - zh)
        return remote(act_block(g), act_block(g), as_.at[o], ar.at[g], at_y((y + o) % NY))

    barrier = pltpu.get_barrier_semaphore()

    def greet(to):
        pl.semaphore_signal(barrier, inc=1, device_id=to, device_id_type=MESH)

    @pl.when(z > 0)
    def _():
        greet(at_z(z - 1))

    @pl.when(z < NZ - 1)
    def _():
        greet(at_z(z + 1))

    for to in (at_x(1), at_x(-1), twin, at_y((y + 1) % NY), at_y((y + 2) % NY), at_y((y + 3) % NY), far):
        greet(to)

    w_copy = pltpu.make_async_copy(w_hbm, w_ref, w_sem)
    w_copy.start()
    rows_all[pl.ds(pl.multiple_of(((z * NX + x) * 2 + c) * BLK, BLK), BLK), :] = g_ref[...]
    pl.semaphore_wait(barrier, 7 + (z > 0).astype(jnp.int32) + (z < NZ - 1).astype(jnp.int32))

    def spread(j):
        x_copy(j, 1).start()
        x_copy(j, 0).start()
        c_copy(j, 0).start()

    @pl.when(z < NZ - 1)
    def _():
        z_copy(z, 1).start()

    @pl.when(z > 0)
    def _():
        z_copy(z, 0).start()

    spread(z)

    hv = h_ref[...].astype(jnp.float32)
    tv = jnp.tanh(coeff * (hv + 0.044715 * hv * hv * hv))
    slope[...] = 0.5 * (1.0 + tv) + 0.5 * hv * (1.0 - tv * tv) * coeff * (1.0 + 3.0 * 0.044715 * hv * hv)
    act = 0.5 * hv * (1.0 + tv)
    act_t[:, pl.ds(pl.multiple_of(gy * TOK, TOK), TOK)] = act.T.astype(jnp.bfloat16)
    for o in (1, 2, 3):
        act_copy(True, o).start()
    w_copy.wait()

    def place(d, side):
        j = jnp.where(side == 0, z - d, z + d)
        valid = (d >= 0) & (d < NZ) & (j >= 0) & (j < NZ) & ((d > 0) | (side == 0))
        return j, valid

    def step(t, carry):
        for side in (0, 1):
            j, valid = place(t, side)

            @pl.when(valid)
            def _():
                z_copy(j, 1).wait_recv()

                @pl.when((z < NZ - 1) if side == 0 else (z > 0))
                def _():
                    z_copy(j, 1 - side).start()

                spread(j)

        @pl.when(t == ACT_SEND)
        def _():
            act_far().start()

        for side in (0, 1):
            j, valid = place(t - 1, side)

            @pl.when(valid)
            def _():
                x_came(j, 1).wait_recv()
                half_copy(j, 1).start()
                c_copy(j, 3).start()
                x_came(j, 0).wait_recv()
                half_copy(j, 0).start()
                c_copy(j, 1).start()

        for side in (0, 1):
            j, valid = place(t - 2, side)

            @pl.when(valid)
            def _():
                half_came(j, 1).wait_recv()
                half_came(j, 0).wait_recv()
                c_copy(j, 2).start()

        def multiply(side, carry):
            j, valid = place(t - 3, side)

            @pl.when(valid)
            def _():
                for o in range(NX):
                    c_came(j, o).wait_recv()
                part[j] = lax.dot_general(
                    rows_all[pl.ds(pl.multiple_of(j * TOK, TOK), TOK), :], w_ref[...],
                    (((1,), (1,)), ((), ())), preferred_element_type=jnp.float32)
                for o in (1, 2, 3):
                    y_copy(j, o).start()

            return carry

        lax.fori_loop(0, 2, multiply, 0)

        def add(side, carry):
            j, valid = place(t - 5, side)

            @pl.when(valid)
            def _():
                for o in (1, 2, 3):
                    y_copy(j, o).wait_recv()
                total = part[j, pl.ds(pl.multiple_of(y * QTR, QTR), QTR), :]
                total = total + from_y[0, j] + from_y[1, j] + from_y[2, j]
                k = j // 2

                @pl.when(j % 2 == zh)
                def _():
                    kept[k] = total

                @pl.when(j % 2 != zh)
                def _():
                    z_out[k] = total.astype(jnp.bfloat16)
                    far_copy(k).start()

            return carry

        lax.fori_loop(0, 2, add, 0)

        @pl.when(t == ACT_PASS)
        def _():
            act_far_came().wait_recv()
            for o in (1, 2, 3):
                act_copy(False, o).start()

        return carry

    lax.fori_loop(1, LAST, step, 0)

    for o in (1, 2, 3):
        act_came(True, o).wait_recv()
    for o in (1, 2, 3):
        act_came(False, o).wait_recv()

    def dw_copy(n):
        cols = pl.ds(pl.multiple_of(n * TILE, TILE), TILE)
        return pltpu.make_async_copy(dw_buf.at[:, cols], dw_hbm.at[:, cols], dw_sem.at[n])

    def weight_tile(n, carry):
        cols = pl.ds(pl.multiple_of(n * TILE, TILE), TILE)
        dw_buf[:, cols] = jnp.dot(act_t[...], rows_all[:, cols], preferred_element_type=jnp.float32)
        dw_copy(n).start()
        return carry

    lax.fori_loop(0, NT, weight_tile, 0)

    def finish(d, carry):
        for side in (0, 1):
            j, valid = place(d, side)

            @pl.when(valid & (j % 2 == zh))
            def _():
                k = j // 2
                far_copy(k).wait_recv()
                total = kept[k] + z_in[k].astype(jnp.float32)

                @pl.when(k == y)
                def _():
                    full[pl.ds(pl.multiple_of(y * QTR, QTR), QTR), :] = total

                @pl.when(k != y)
                def _():
                    kept[k] = total
                    full_copy(k).start()

        return carry

    lax.fori_loop(0, NZ, finish, 0)
    for o in (1, 2, 3):
        full_came(o).wait_recv()
    gh_ref[...] = (full[...] * slope[...]).astype(jnp.bfloat16)

    def sent(j, carry):
        @pl.when((z < NZ - 1) & (j <= z))
        def _():
            z_copy(j, 1).wait_send()

        @pl.when((z > 0) & (j >= z))
        def _():
            z_copy(j, 0).wait_send()

        for up in (0, 1):
            x_copy(j, up).wait_send()
            half_copy(j, up).wait_send()
        for o in range(NX):
            c_copy(j, o).wait_send()
        for o in (1, 2, 3):
            y_copy(j, o).wait_send()
        return carry

    lax.fori_loop(0, NZ, sent, 0)
    act_far().wait_send()
    for o in (1, 2, 3):
        act_copy(True, o).wait_send()
        act_copy(False, o).wait_send()

    def sent_sums(k, carry):
        far_copy(k).wait_send()

        @pl.when(k != y)
        def _():
            full_copy(k).wait_send()

        return carry

    lax.fori_loop(0, NY, sent_sums, 0)

    def stored(n, carry):
        dw_copy(n).wait()
        return carry

    lax.fori_loop(0, NT, stored, 0)


def body(hidden_pre, grad_out, down_weight):
    vmem = pl.BlockSpec(memory_space=pltpu.VMEM)
    hbm = pl.BlockSpec(memory_space=pl.ANY)
    dma = pltpu.SemaphoreType.DMA
    return pl.pallas_call(
        kernel,
        name="ffn_backward",
        out_shape=(jax.ShapeDtypeStruct((TOK, HID), jnp.bfloat16), jax.ShapeDtypeStruct((HID, FEAT), jnp.float32)),
        in_specs=[vmem, vmem, hbm],
        out_specs=(vmem, hbm),
        scratch_shapes=[
            pltpu.VMEM((NZ * TOK, FEAT), jnp.bfloat16),
            pltpu.VMEM((HID, FEAT), jnp.bfloat16),
            pltpu.VMEM((HID, NZ * TOK), jnp.bfloat16),
            pltpu.VMEM((TOK, HID), jnp.float32),
            pltpu.VMEM((NZ, TOK, HID), jnp.float32),
            pltpu.VMEM((NY - 1, NZ, QTR, HID), jnp.float32),
            pltpu.VMEM((NY, QTR, HID), jnp.float32),
            pltpu.VMEM((NY, QTR, HID), jnp.bfloat16),
            pltpu.VMEM((NY, QTR, HID), jnp.bfloat16),
            pltpu.VMEM((TOK, HID), jnp.float32),
            pltpu.VMEM((HID, FEAT), jnp.float32),
            dma, dma((NT,)),
            dma((2, NZ)), dma((NZ,)),
            dma((2, NZ)), dma((2, NZ)),
            dma((2, NZ)), dma((2, NZ)),
            dma((NX, NZ)), dma((NX, NZ)),
            dma((NY - 1, NZ)), dma((NY - 1, NZ)),
            dma((NY,)), dma((NY,)),
            dma((7,)), dma((NZ,)),
            dma((NY,)), dma((NY,)),
        ],
        compiler_params=pltpu.CompilerParams(
            collective_id=0, has_side_effects=True, vmem_limit_bytes=48 * 1024 * 1024),
        cost_estimate=pl.CostEstimate(flops=4 * 2048 * 1536 * 384, bytes_accessed=12 << 20, transcendentals=256 * 384),
    )(hidden_pre, grad_out, down_weight)


def solution(mesh):
    placed = (P("gy", ("gz", "gx")), P(("gx", "gz"), "gy"), P(("gz", "gx"), "gy"))
    return jax.shard_map(
        body,
        mesh=mesh,
        in_specs=placed,
        out_specs=(P("gy", ("gz", "gx")), P(("gz", "gx"), "gy")),
        check_vma=False,
    )
```

```python
import math

import jax
import jax.numpy as jnp
from jax import lax
from jax.experimental import pallas as pl
from jax.experimental.pallas import tpu as pltpu
from jax.sharding import PartitionSpec as P

MESH = pl.DeviceIdType.MESH
coeff = math.sqrt(2.0 / math.pi)

NZ, NY, NX = 8, 4, 4
BLK = 32
TOK = 256
QTR = TOK // NY
FEAT = 1536
HID = 384
TILE = 256
NT = FEAT // TILE
PARTS = 4
PIECE = HID // PARTS
ACT_SEND, ACT_PASS = 0, 4
LAG_MUL, LAG_ADD = 3, 5
LAST = 13
NAME = "ffn_backward"
Y_TYPE = jnp.bfloat16
VMEM_MB = 60
ORDER = [(p % NX) * 2 + p // NX for p in range(8)]


def kernel(h_hbm, g_hbm, w_hbm, gh_ref, dw_hbm,
           rows_all, h_ref, h_part, w_ref, act_t, product, part, mine, from_y, kept, z_out, z_in, own, full, dw_buf,
           in_sem, dw_sem, zs, zr, xs, xr, hs, hr, cs, cr, ys, yr, ts, tr, as_, ar, aos, aor, aps, apr, fs, fr, hqs, hqr):
    gx, gy, gz = lax.axis_index("gx"), lax.axis_index("gy"), lax.axis_index("gz")
    y, zh = gy // 2, gy % 2
    x, c = gz // 2, gz % 2
    z = gx

    def at_z(v):
        return {"gx": v, "gy": gy, "gz": gz}

    def at_x(o):
        return {"gx": gx, "gy": gy, "gz": ((x + o) % NX) * 2 + c}

    def at_y(v):
        return {"gx": gx, "gy": v * 2 + zh, "gz": gz}

    twin = {"gx": gx, "gy": gy, "gz": x * 2 + (1 - c)}
    far = {"gx": gx, "gy": y * 2 + (1 - zh), "gz": gz}

    def block(j, xx, cc, start=0, size=BLK):
        return rows_all.at[pl.ds(pl.multiple_of(((j * 2 + cc) * NX + xx) * BLK + start, 16), size)]

    def remote(src, dst, send, recv, to):
        return pltpu.make_async_remote_copy(
            src_ref=src, dst_ref=dst, send_sem=send, recv_sem=recv, device_id=to, device_id_type=MESH)

    def z_copy(j, up, half):
        b = block(j, x, c, half * 16, 16)
        return remote(b, b, zs.at[up, j, half], zr.at[j, half], at_z(z + 1 if up else z - 1))

    def x_copy(j, up):
        b = block(j, x, c)
        return remote(b, b, xs.at[up, j], xr.at[up, j], at_x(1 if up else -1))

    def x_came(j, up):
        b = block(j, (x + (NX - 1 if up else 1)) % NX, c)
        return remote(b, b, xs.at[up, j], xr.at[up, j], at_x(1 if up else -1))

    def half_copy(j, up):
        b = block(j, (x + (NX - 1 if up else 1)) % NX, c, 0 if up else 16, 16)
        return remote(b, b, hs.at[up, j], hr.at[up, j], at_x(1 if up else -1))

    def half_came(j, up):
        b = block(j, (x + 2) % NX, c, 0 if up else 16, 16)
        return remote(b, b, hs.at[up, j], hr.at[up, j], at_x(1 if up else -1))

    def half_of_place(j, cc):
        return rows_all.at[pl.ds(pl.multiple_of((j * 2 + cc) * NX * BLK, NX * BLK), NX * BLK)]

    def c_copy(j):
        b = half_of_place(j, c)
        return remote(b, b, cs.at[j], cr.at[j], twin)

    def c_came(j):
        b = half_of_place(j, 1 - c)
        return remote(b, b, cs.at[j], cr.at[j], twin)

    def y_copy(j, o):
        yt = (y + o) % NY
        return remote(part.at[j, pl.ds(pl.multiple_of(yt * QTR, QTR), QTR)], from_y.at[o - 1, j],
                      ys.at[o - 1, j], yr.at[o - 1, j], at_y(yt))

    def far_copy(k):
        return remote(z_out.at[k], z_in.at[k], ts.at[k], tr.at[k], far)

    def full_copy(k):
        return remote(own.at[k], full.at[pl.ds(pl.multiple_of(y * QTR, QTR), QTR)], fs.at[k], fr.at[y], at_y(k))

    def full_came(o):
        yt = (y + o) % NY
        return remote(own.at[yt], full.at[pl.ds(pl.multiple_of(yt * QTR, QTR), QTR)], fs.at[yt], fr.at[yt], at_y(yt))

    def h_copy_to(o):
        yt = (y + o) % NY
        return remote(h_ref.at[pl.ds(pl.multiple_of(yt * QTR, QTR), QTR)], h_part.at[y], hqs.at[o - 1], hqr.at[o - 1], at_y(yt))

    def h_came(o):
        return remote(h_part.at[y], h_part.at[(y + NY - o) % NY], hqs.at[o - 1], hqr.at[o - 1], at_y((y + o) % NY))

    def act_block(g, q=None):
        rows = pl.ds(0, HID) if q is None else pl.ds(q * PIECE, PIECE)
        return act_t.at[rows, pl.ds(pl.multiple_of(g * TOK, TOK), TOK)]

    other = y * 2 + 1 - zh

    def act_far(q):
        return remote(act_block(gy, q), act_block(gy, q), as_.at[q], ar.at[q], far)

    def act_far_came(q):
        return remote(act_block(other, q), act_block(other, q), as_.at[q], ar.at[q], far)

    def act_copy(o):
        return remote(act_block(gy), act_block(gy), aos.at[o - 1], aor.at[o - 1], at_y((y + o) % NY))

    def act_came(o):
        b = act_block(((y + NY - o) % NY) * 2 + zh)
        return remote(b, b, aos.at[o - 1], aor.at[o - 1], at_y((y + o) % NY))

    def act_pass(o, q):
        return remote(act_block(other, q), act_block(other, q), aps.at[o - 1, q], apr.at[o - 1, q], at_y((y + o) % NY))

    def act_passed(o, q):
        b = act_block(((y + NY - o) % NY) * 2 + 1 - zh, q)
        return remote(b, b, aps.at[o - 1, q], apr.at[o - 1, q], at_y((y + o) % NY))

    barrier = pltpu.get_barrier_semaphore()

    def greet(to):
        pl.semaphore_signal(barrier, inc=1, device_id=to, device_id_type=MESH)

    @pl.when(z > 0)
    def _():
        greet(at_z(z - 1))

    @pl.when(z < NZ - 1)
    def _():
        greet(at_z(z + 1))

    for to in (at_x(1), at_x(-1), twin, at_y((y + 1) % NY), at_y((y + 2) % NY), at_y((y + 3) % NY), far):
        greet(to)

    g_copy = pltpu.make_async_copy(g_hbm, block(z, x, c), in_sem.at[0])
    h_copies = [pltpu.make_async_copy(h_hbm.at[pl.ds(q * BLK, BLK)], h_ref.at[pl.ds(p * BLK, BLK)], in_sem.at[2 + p])
                for p, q in enumerate(ORDER)]
    w_copy = pltpu.make_async_copy(w_hbm, w_ref, in_sem.at[1])
    g_copy.start()
    for h_copy in h_copies:
        h_copy.start()
    w_copy.start()
    g_copy.wait()
    pl.semaphore_wait(barrier, 7 + (z > 0).astype(jnp.int32) + (z < NZ - 1).astype(jnp.int32))

    def spread(j):
        x_copy(j, 1).start()
        x_copy(j, 0).start()

    for half in (0, 1):
        @pl.when(z < NZ - 1)
        def _():
            z_copy(z, 1, half).start()

        @pl.when(z > 0)
        def _():
            z_copy(z, 0, half).start()

    spread(z)

    for h_copy in h_copies:
        h_copy.wait()
    for o in (1, 2, 3):
        h_copy_to(o).start()
    h_part[y] = h_ref[pl.ds(pl.multiple_of(y * QTR, QTR), QTR), :]
    hv = h_ref[...].astype(jnp.float32)
    act = 0.5 * hv * (1.0 + jnp.tanh(coeff * (hv + 0.044715 * hv * hv * hv)))
    act_t[:, pl.ds(pl.multiple_of(gy * TOK, TOK), TOK)] = act.T.astype(jnp.bfloat16)
    for o in (1, 2, 3):
        act_copy(o).start()
    for q in range(PARTS):
        if ACT_SEND + q <= 0:
            act_far(q).start()
    w_copy.wait()

    def place(d, side):
        j = jnp.where(side == 0, z - d, z + d)
        valid = (d >= 0) & (d < NZ) & (j >= 0) & (j < NZ) & ((d > 0) | (side == 0))
        return j, valid

    def step(t, carry):
        for half in (0, 1):
            for side in (0, 1):
                j, valid = place(t, side)

                @pl.when(valid)
                def _():
                    z_copy(j, 1, half).wait_recv()

                    @pl.when((z < NZ - 1) if side == 0 else (z > 0))
                    def _():
                        z_copy(j, 1 - side, half).start()

        for side in (0, 1):
            j, valid = place(t, side)

            @pl.when(valid)
            def _():
                spread(j)

        for q in range(PARTS):
            if ACT_SEND + q > 0:
                @pl.when(t == ACT_SEND + q)
                def _():
                    act_far(q).start()

        for side in (0, 1):
            j, valid = place(t - 1, side)

            @pl.when(valid)
            def _():
                x_came(j, 1).wait_recv()
                half_copy(j, 1).start()
                x_came(j, 0).wait_recv()
                half_copy(j, 0).start()

        for side in (0, 1):
            j, valid = place(t - 2, side)

            @pl.when(valid)
            def _():
                half_came(j, 1).wait_recv()
                half_came(j, 0).wait_recv()
                c_copy(j).start()

        def multiply(side, carry):
            j, valid = place(t - LAG_MUL, side)

            @pl.when(valid)
            def _():
                c_came(j).wait_recv()
                product[...] = lax.dot_general(
                    rows_all[pl.ds(pl.multiple_of(j * TOK, TOK), TOK), :], w_ref[...],
                    (((1,), (1,)), ((), ())), preferred_element_type=jnp.float32)
                part[j] = product[...].astype(part.dtype)
                mine[j] = product[pl.ds(pl.multiple_of(y * QTR, QTR), QTR), :]
                for o in (1, 2, 3):
                    y_copy(j, o).start()

            return carry

        lax.fori_loop(0, 2, multiply, 0)

        def add(side, carry):
            j, valid = place(t - LAG_ADD, side)

            @pl.when(valid)
            def _():
                for o in (1, 2, 3):
                    y_copy(j, o).wait_recv()
                total = mine[j]
                for o in (0, 1, 2):
                    total = total + from_y[o, j].astype(jnp.float32)
                k = j // 2

                @pl.when(j % 2 == zh)
                def _():
                    kept[k] = total

                @pl.when(j % 2 != zh)
                def _():
                    z_out[k] = total.astype(jnp.bfloat16)
                    far_copy(k).start()

            return carry

        lax.fori_loop(0, 2, add, 0)

        for q in range(PARTS):
            if ACT_PASS + q < LAST:
                @pl.when(t == ACT_PASS + q)
                def _():
                    act_far_came(q).wait_recv()
                    for o in (1, 2, 3):
                        act_pass(o, q).start()

        return carry

    lax.fori_loop(1, LAST, step, 0)

    def dw_copy(n):
        cols = pl.ds(pl.multiple_of(n * TILE, TILE), TILE)
        return pltpu.make_async_copy(dw_buf.at[:, cols], dw_hbm.at[:, cols], dw_sem.at[n])

    def weight_tile(n, carry):
        cols = pl.ds(pl.multiple_of(n * TILE, TILE), TILE)
        dw_buf[:, cols] = jnp.dot(act_t[...], rows_all[:, cols], preferred_element_type=jnp.float32)
        dw_copy(n).start()
        return carry


    def finish(d, carry):
        for side in (0, 1):
            j, valid = place(d, side)

            @pl.when(valid & (j % 2 == zh))
            def _():
                k = j // 2
                far_copy(k).wait_recv()
                grad_act = kept[k] + z_in[k].astype(jnp.float32)
                hk = h_part[k].astype(jnp.float32)
                tk = jnp.tanh(coeff * (hk + 0.044715 * hk * hk * hk))
                slope = 0.5 * (1.0 + tk) + 0.5 * hk * (1.0 - tk * tk) * coeff * (1.0 + 3.0 * 0.044715 * hk * hk)
                result = (grad_act * slope).astype(jnp.bfloat16)

                @pl.when(k == y)
                def _():
                    full[pl.ds(pl.multiple_of(y * QTR, QTR), QTR), :] = result

                @pl.when(k != y)
                def _():
                    own[k] = result
                    full_copy(k).start()

        return carry

    for o in (1, 2, 3):
        h_came(o).wait_recv()
    lax.fori_loop(0, NZ, finish, 0)

    for q in range(PARTS):
        if ACT_PASS + q >= LAST:
            act_far_came(q).wait_recv()
            for o in (1, 2, 3):
                act_pass(o, q).start()
    for o in (1, 2, 3):
        act_came(o).wait_recv()
        for q in range(PARTS):
            act_passed(o, q).wait_recv()

    lax.fori_loop(0, NT, weight_tile, 0)

    def sent(j, carry):
        for half in (0, 1):
            @pl.when((z < NZ - 1) & (j <= z))
            def _():
                z_copy(j, 1, half).wait_send()

            @pl.when((z > 0) & (j >= z))
            def _():
                z_copy(j, 0, half).wait_send()

        for up in (0, 1):
            x_copy(j, up).wait_send()
            half_copy(j, up).wait_send()
        c_copy(j).wait_send()
        for o in (1, 2, 3):
            y_copy(j, o).wait_send()
        return carry

    lax.fori_loop(0, NZ, sent, 0)
    for q in range(PARTS):
        act_far(q).wait_send()
    for o in (1, 2, 3):
        act_copy(o).wait_send()
        for q in range(PARTS):
            act_pass(o, q).wait_send()

    for o in (1, 2, 3):
        h_copy_to(o).wait_send()

    def sent_sums(k, carry):
        far_copy(k).wait_send()

        @pl.when(k != y)
        def _():
            full_copy(k).wait_send()

        return carry

    lax.fori_loop(0, NY, sent_sums, 0)

    for o in (1, 2, 3):
        full_came(o).wait_recv()
    for p, q in enumerate(ORDER):
        rows = slice(p * BLK, (p + 1) * BLK)
        gh_ref[q * BLK:(q + 1) * BLK, :] = full[rows, :]

    def stored(n, carry):
        dw_copy(n).wait()
        return carry

    lax.fori_loop(0, NT, stored, 0)


def body(hidden_pre, grad_out, down_weight):
    vmem = pl.BlockSpec(memory_space=pltpu.VMEM)
    hbm = pl.BlockSpec(memory_space=pl.ANY)
    dma = pltpu.SemaphoreType.DMA
    return pl.pallas_call(
        kernel,
        name=NAME,
        out_shape=(pltpu.VMEM((TOK, HID), jnp.bfloat16), pltpu.VMEM((HID, FEAT), jnp.float32)),
        in_specs=[hbm, hbm, hbm],
        out_specs=(vmem, hbm),
        scratch_shapes=[
            pltpu.VMEM((NZ * TOK, FEAT), jnp.bfloat16),
            pltpu.VMEM((TOK, HID), jnp.bfloat16),
            pltpu.VMEM((NY, QTR, HID), jnp.bfloat16),
            pltpu.VMEM((HID, FEAT), jnp.bfloat16),
            pltpu.VMEM((HID, NZ * TOK), jnp.bfloat16),
            pltpu.VMEM((TOK, HID), jnp.float32),
            pltpu.VMEM((NZ, TOK, HID), Y_TYPE),
            pltpu.VMEM((NZ, QTR, HID), jnp.float32),
            pltpu.VMEM((NY - 1, NZ, QTR, HID), Y_TYPE),
            pltpu.VMEM((NY, QTR, HID), jnp.float32),
            pltpu.VMEM((NY, QTR, HID), jnp.bfloat16),
            pltpu.VMEM((NY, QTR, HID), jnp.bfloat16),
            pltpu.VMEM((NY, QTR, HID), jnp.bfloat16),
            pltpu.VMEM((TOK, HID), jnp.bfloat16),
            pltpu.VMEM((HID, FEAT), jnp.float32),
            dma((10,)), dma((NT,)),
            dma((2, NZ, 2)), dma((NZ, 2)),
            dma((2, NZ)), dma((2, NZ)),
            dma((2, NZ)), dma((2, NZ)),
            dma((NZ,)), dma((NZ,)),
            dma((NY - 1, NZ)), dma((NY - 1, NZ)),
            dma((NY,)), dma((NY,)),
            dma((PARTS,)), dma((PARTS,)), dma((NY - 1,)), dma((NY - 1,)),
            dma((NY - 1, PARTS)), dma((NY - 1, PARTS)),
            dma((NY,)), dma((NY,)),
            dma((NY - 1,)), dma((NY - 1,)),
        ],
        compiler_params=pltpu.CompilerParams(
            collective_id=0, has_side_effects=True, vmem_limit_bytes=VMEM_MB * 1024 * 1024),
        cost_estimate=pl.CostEstimate(flops=4 * 2048 * 1536 * 384, bytes_accessed=12 << 20, transcendentals=256 * 384),
    )(hidden_pre, grad_out, down_weight)


def solution(mesh):
    placed = (P("gy", ("gz", "gx")), P(("gx", "gz"), "gy"), P(("gz", "gx"), "gy"))
    return jax.shard_map(
        body,
        mesh=mesh,
        in_specs=placed,
        out_specs=(P("gy", ("gz", "gx")), P(("gz", "gx"), "gy")),
        check_vma=False,
    )
```

```python
import math

import jax
import jax.numpy as jnp
from jax import lax
from jax.experimental import pallas as pl
from jax.experimental.pallas import tpu as pltpu
from jax.sharding import PartitionSpec as P

MESH = pl.DeviceIdType.MESH
coeff = math.sqrt(2.0 / math.pi)

NZ, NY, NX = 8, 4, 4
BLK = 32
TOK = 256
QTR = TOK // NY
FEAT = 1536
HID = 384
TILE = 256
NT = FEAT // TILE
PARTS = 4
PIECE = HID // PARTS
ACT_SEND, ACT_PASS = (0, 1), 4
LAG_X, LAG_HALF, LAG_MUL, LAG_ADD = 1, 2, 3, 5
LAST = 13
NAME = "ffn_backward"
Y_TYPE = jnp.bfloat16
VMEM_MB = 60
ORDER = [(p % NX) * 2 + p // NX for p in range(8)]


def kernel(h_hbm, g_hbm, w_hbm, gh_ref, dw_hbm,
           rows_all, h_ref, h_part, w_ref, act_t, product, part, mine, from_y, kept, z_out, z_in, own, full, dw_buf,
           in_sem, dw_sem, zs, zr, xs, xr, hs, hr, cs, cr, ys, yr, ts, tr, as_, ar, aos, aor, aps, apr, fs, fr, hqs, hqr):
    gx, gy, gz = lax.axis_index("gx"), lax.axis_index("gy"), lax.axis_index("gz")
    y, zh = gy // 2, gy % 2
    x, c = gz // 2, gz % 2
    z = gx

    def at_z(v):
        return {"gx": v, "gy": gy, "gz": gz}

    def at_x(o):
        return {"gx": gx, "gy": gy, "gz": ((x + o) % NX) * 2 + c}

    def at_y(v):
        return {"gx": gx, "gy": v * 2 + zh, "gz": gz}

    twin = {"gx": gx, "gy": gy, "gz": x * 2 + (1 - c)}
    far = {"gx": gx, "gy": y * 2 + (1 - zh), "gz": gz}

    def block(j, xx, cc, start=0, size=BLK):
        return rows_all.at[pl.ds(pl.multiple_of(((j * 2 + cc) * NX + xx) * BLK + start, 16), size)]

    def remote(src, dst, send, recv, to):
        return pltpu.make_async_remote_copy(
            src_ref=src, dst_ref=dst, send_sem=send, recv_sem=recv, device_id=to, device_id_type=MESH)

    def z_copy(j, up, half):
        b = block(j, x, c, half * 16, 16)
        return remote(b, b, zs.at[up, j, half], zr.at[j, half], at_z(z + 1 if up else z - 1))

    def x_copy(j, up, half):
        b = block(j, x, c, half * 16, 16)
        return remote(b, b, xs.at[up, j, half], xr.at[up, j, half], at_x(1 if up else -1))

    def x_came(j, up, half):
        b = block(j, (x + (NX - 1 if up else 1)) % NX, c, half * 16, 16)
        return remote(b, b, xs.at[up, j, half], xr.at[up, j, half], at_x(1 if up else -1))

    def half_copy(j, up):
        b = block(j, (x + (NX - 1 if up else 1)) % NX, c, 0 if up else 16, 16)
        return remote(b, b, hs.at[up, j], hr.at[up, j], at_x(1 if up else -1))

    def half_came(j, up):
        b = block(j, (x + 2) % NX, c, 0 if up else 16, 16)
        return remote(b, b, hs.at[up, j], hr.at[up, j], at_x(1 if up else -1))

    def half_of_place(j, cc):
        return rows_all.at[pl.ds(pl.multiple_of((j * 2 + cc) * NX * BLK, NX * BLK), NX * BLK)]

    def c_copy(j):
        b = half_of_place(j, c)
        return remote(b, b, cs.at[j], cr.at[j], twin)

    def c_came(j):
        b = half_of_place(j, 1 - c)
        return remote(b, b, cs.at[j], cr.at[j], twin)

    def y_copy(j, o):
        yt = (y + o) % NY
        return remote(part.at[j, pl.ds(pl.multiple_of(yt * QTR, QTR), QTR)], from_y.at[o - 1, j],
                      ys.at[o - 1, j], yr.at[o - 1, j], at_y(yt))

    def far_copy(k):
        return remote(z_out.at[k], z_in.at[k], ts.at[k], tr.at[k], far)

    def full_copy(k):
        return remote(own.at[k], full.at[pl.ds(pl.multiple_of(y * QTR, QTR), QTR)], fs.at[k], fr.at[y], at_y(k))

    def full_came(o):
        yt = (y + o) % NY
        return remote(own.at[yt], full.at[pl.ds(pl.multiple_of(yt * QTR, QTR), QTR)], fs.at[yt], fr.at[yt], at_y(yt))

    def h_copy_to(o):
        yt = (y + o) % NY
        return remote(h_ref.at[pl.ds(pl.multiple_of(yt * QTR, QTR), QTR)], h_part.at[y], hqs.at[o - 1], hqr.at[o - 1], at_y(yt))

    def h_came(o):
        return remote(h_part.at[y], h_part.at[(y + NY - o) % NY], hqs.at[o - 1], hqr.at[o - 1], at_y((y + o) % NY))

    def act_block(g, q=None):
        rows = pl.ds(0, HID) if q is None else pl.ds(q * PIECE, PIECE)
        return act_t.at[rows, pl.ds(pl.multiple_of(g * TOK, TOK), TOK)]

    other = y * 2 + 1 - zh

    def act_far(q):
        return remote(act_block(gy, q), act_block(gy, q), as_.at[q], ar.at[q], far)

    def act_far_came(q):
        return remote(act_block(other, q), act_block(other, q), as_.at[q], ar.at[q], far)

    def act_copy(o):
        return remote(act_block(gy), act_block(gy), aos.at[o - 1], aor.at[o - 1], at_y((y + o) % NY))

    def act_came(o):
        b = act_block(((y + NY - o) % NY) * 2 + zh)
        return remote(b, b, aos.at[o - 1], aor.at[o - 1], at_y((y + o) % NY))

    def act_pass(o, q):
        return remote(act_block(other, q), act_block(other, q), aps.at[o - 1, q], apr.at[o - 1, q], at_y((y + o) % NY))

    def act_passed(o, q):
        b = act_block(((y + NY - o) % NY) * 2 + 1 - zh, q)
        return remote(b, b, aps.at[o - 1, q], apr.at[o - 1, q], at_y((y + o) % NY))

    barrier = pltpu.get_barrier_semaphore()

    def greet(to):
        pl.semaphore_signal(barrier, inc=1, device_id=to, device_id_type=MESH)

    @pl.when(z > 0)
    def _():
        greet(at_z(z - 1))

    @pl.when(z < NZ - 1)
    def _():
        greet(at_z(z + 1))

    for to in (at_x(1), at_x(-1), twin, at_y((y + 1) % NY), at_y((y + 2) % NY), at_y((y + 3) % NY), far):
        greet(to)

    g_copy = pltpu.make_async_copy(g_hbm, block(z, x, c), in_sem.at[0])
    h_copies = [pltpu.make_async_copy(h_hbm.at[pl.ds(q * BLK, BLK)], h_ref.at[pl.ds(p * BLK, BLK)], in_sem.at[2 + p])
                for p, q in enumerate(ORDER)]
    w_copy = pltpu.make_async_copy(w_hbm, w_ref, in_sem.at[1])
    g_copy.start()
    for h_copy in h_copies:
        h_copy.start()
    w_copy.start()
    g_copy.wait()
    pl.semaphore_wait(barrier, 7 + (z > 0).astype(jnp.int32) + (z < NZ - 1).astype(jnp.int32))

    def spread(j):
        x_copy(j, 1, 0).start()
        x_copy(j, 0, 1).start()
        x_copy(j, 1, 1).start()
        x_copy(j, 0, 0).start()

    for half in (0, 1):
        @pl.when(z < NZ - 1)
        def _():
            z_copy(z, 1, half).start()

        @pl.when(z > 0)
        def _():
            z_copy(z, 0, half).start()

    spread(z)

    for h_copy in h_copies:
        h_copy.wait()
    for o in (1, 2, 3):
        h_copy_to(o).start()
    h_part[y] = h_ref[pl.ds(pl.multiple_of(y * QTR, QTR), QTR), :]
    hv = h_ref[...].astype(jnp.float32)
    act = 0.5 * hv * (1.0 + jnp.tanh(coeff * (hv + 0.044715 * hv * hv * hv)))
    act_t[:, pl.ds(pl.multiple_of(gy * TOK, TOK), TOK)] = act.T.astype(jnp.bfloat16)
    for o in (1, 2, 3):
        act_copy(o).start()
    act_send = jnp.where(zh == 0, ACT_SEND[0], ACT_SEND[1])
    for q in range(PARTS):
        @pl.when(act_send + q <= 0)
        def _():
            act_far(q).start()
    w_copy.wait()

    def place(d, side):
        j = jnp.where(side == 0, z - d, z + d)
        valid = (d >= 0) & (d < NZ) & (j >= 0) & (j < NZ) & ((d > 0) | (side == 0))
        return j, valid

    def step(t, carry):
        for half in (0, 1):
            for side in (0, 1):
                j, valid = place(t, side)

                @pl.when(valid)
                def _():
                    z_copy(j, 1, half).wait_recv()

                    @pl.when((z < NZ - 1) if side == 0 else (z > 0))
                    def _():
                        z_copy(j, 1 - side, half).start()

        for side in (0, 1):
            j, valid = place(t, side)

            @pl.when(valid)
            def _():
                spread(j)

        for q in range(PARTS):
            @pl.when(t == act_send + q)
            def _():
                act_far(q).start()

        for side in (0, 1):
            j, valid = place(t - LAG_X, side)

            @pl.when(valid)
            def _():
                x_came(j, 1, 0).wait_recv()
                half_copy(j, 1).start()
                x_came(j, 0, 1).wait_recv()
                half_copy(j, 0).start()

        for side in (0, 1):
            j, valid = place(t - LAG_HALF, side)

            @pl.when(valid)
            def _():
                x_came(j, 1, 1).wait_recv()
                x_came(j, 0, 0).wait_recv()
                half_came(j, 1).wait_recv()
                half_came(j, 0).wait_recv()
                c_copy(j).start()

        def multiply(side, carry):
            j, valid = place(t - LAG_MUL, side)

            @pl.when(valid)
            def _():
                c_came(j).wait_recv()
                product[...] = lax.dot_general(
                    rows_all[pl.ds(pl.multiple_of(j * TOK, TOK), TOK), :], w_ref[...],
                    (((1,), (1,)), ((), ())), preferred_element_type=jnp.float32)
                part[j] = product[...].astype(part.dtype)
                mine[j] = product[pl.ds(pl.multiple_of(y * QTR, QTR), QTR), :]
                for o in (1, 2, 3):
                    y_copy(j, o).start()

            return carry

        lax.fori_loop(0, 2, multiply, 0)

        def add(side, carry):
            j, valid = place(t - LAG_ADD, side)

            @pl.when(valid)
            def _():
                for o in (1, 2, 3):
                    y_copy(j, o).wait_recv()
                total = mine[j]
                for o in (0, 1, 2):
                    total = total + from_y[o, j].astype(jnp.float32)
                k = j // 2

                @pl.when(j % 2 == zh)
                def _():
                    kept[k] = total

                @pl.when(j % 2 != zh)
                def _():
                    z_out[k] = total.astype(jnp.bfloat16)
                    far_copy(k).start()

            return carry

        lax.fori_loop(0, 2, add, 0)

        for q in range(PARTS):
            @pl.when(t == ACT_PASS + q)
            def _():
                act_far_came(q).wait_recv()
                for o in (1, 2, 3):
                    act_pass(o, q).start()

        return carry

    lax.fori_loop(1, LAST, step, 0)

    def dw_copy(n):
        cols = pl.ds(pl.multiple_of(n * TILE, TILE), TILE)
        return pltpu.make_async_copy(dw_buf.at[:, cols], dw_hbm.at[:, cols], dw_sem.at[n])

    def weight_tile(n, carry):
        cols = pl.ds(pl.multiple_of(n * TILE, TILE), TILE)
        dw_buf[:, cols] = jnp.dot(act_t[...], rows_all[:, cols], preferred_element_type=jnp.float32)
        dw_copy(n).start()
        return carry


    def finish(d, carry):
        for side in (0, 1):
            j, valid = place(d, side)

            @pl.when(valid & (j % 2 == zh))
            def _():
                k = j // 2
                far_copy(k).wait_recv()
                grad_act = kept[k] + z_in[k].astype(jnp.float32)
                hk = h_part[k].astype(jnp.float32)
                tk = jnp.tanh(coeff * (hk + 0.044715 * hk * hk * hk))
                slope = 0.5 * (1.0 + tk) + 0.5 * hk * (1.0 - tk * tk) * coeff * (1.0 + 3.0 * 0.044715 * hk * hk)
                result = (grad_act * slope).astype(jnp.bfloat16)

                @pl.when(k == y)
                def _():
                    full[pl.ds(pl.multiple_of(y * QTR, QTR), QTR), :] = result

                @pl.when(k != y)
                def _():
                    own[k] = result
                    full_copy(k).start()

        return carry

    for o in (1, 2, 3):
        h_came(o).wait_recv()
        act_came(o).wait_recv()

    lax.fori_loop(0, NZ, finish, 0)
    for o in (1, 2, 3):
        for q in range(PARTS):
            act_passed(o, q).wait_recv()
    lax.fori_loop(0, NT, weight_tile, 0)

    def sent(j, carry):
        for half in (0, 1):
            @pl.when((z < NZ - 1) & (j <= z))
            def _():
                z_copy(j, 1, half).wait_send()

            @pl.when((z > 0) & (j >= z))
            def _():
                z_copy(j, 0, half).wait_send()

        for up in (0, 1):
            x_copy(j, up, 0).wait_send()
            x_copy(j, up, 1).wait_send()
            half_copy(j, up).wait_send()
        c_copy(j).wait_send()
        for o in (1, 2, 3):
            y_copy(j, o).wait_send()
        return carry

    lax.fori_loop(0, NZ, sent, 0)
    for q in range(PARTS):
        act_far(q).wait_send()
    for o in (1, 2, 3):
        act_copy(o).wait_send()
        for q in range(PARTS):
            act_pass(o, q).wait_send()

    for o in (1, 2, 3):
        h_copy_to(o).wait_send()

    def sent_sums(k, carry):
        far_copy(k).wait_send()

        @pl.when(k != y)
        def _():
            full_copy(k).wait_send()

        return carry

    lax.fori_loop(0, NY, sent_sums, 0)

    for o in (1, 2, 3):
        full_came(o).wait_recv()
    for p, q in enumerate(ORDER):
        rows = slice(p * BLK, (p + 1) * BLK)
        gh_ref[q * BLK:(q + 1) * BLK, :] = full[rows, :]

    def stored(n, carry):
        dw_copy(n).wait()
        return carry

    lax.fori_loop(0, NT, stored, 0)


def body(hidden_pre, grad_out, down_weight):
    vmem = pl.BlockSpec(memory_space=pltpu.VMEM)
    hbm = pl.BlockSpec(memory_space=pl.ANY)
    dma = pltpu.SemaphoreType.DMA
    return pl.pallas_call(
        kernel,
        name=NAME,
        out_shape=(pltpu.VMEM((TOK, HID), jnp.bfloat16), pltpu.VMEM((HID, FEAT), jnp.float32)),
        in_specs=[hbm, hbm, hbm],
        out_specs=(vmem, hbm),
        scratch_shapes=[
            pltpu.VMEM((NZ * TOK, FEAT), jnp.bfloat16),
            pltpu.VMEM((TOK, HID), jnp.bfloat16),
            pltpu.VMEM((NY, QTR, HID), jnp.bfloat16),
            pltpu.VMEM((HID, FEAT), jnp.bfloat16),
            pltpu.VMEM((HID, NZ * TOK), jnp.bfloat16),
            pltpu.VMEM((TOK, HID), jnp.float32),
            pltpu.VMEM((NZ, TOK, HID), Y_TYPE),
            pltpu.VMEM((NZ, QTR, HID), jnp.float32),
            pltpu.VMEM((NY - 1, NZ, QTR, HID), Y_TYPE),
            pltpu.VMEM((NY, QTR, HID), jnp.float32),
            pltpu.VMEM((NY, QTR, HID), jnp.bfloat16),
            pltpu.VMEM((NY, QTR, HID), jnp.bfloat16),
            pltpu.VMEM((NY, QTR, HID), jnp.bfloat16),
            pltpu.VMEM((TOK, HID), jnp.bfloat16),
            pltpu.VMEM((HID, FEAT), jnp.float32),
            dma((10,)), dma((NT,)),
            dma((2, NZ, 2)), dma((NZ, 2)),
            dma((2, NZ, 2)), dma((2, NZ, 2)),
            dma((2, NZ)), dma((2, NZ)),
            dma((NZ,)), dma((NZ,)),
            dma((NY - 1, NZ)), dma((NY - 1, NZ)),
            dma((NY,)), dma((NY,)),
            dma((PARTS,)), dma((PARTS,)), dma((NY - 1,)), dma((NY - 1,)),
            dma((NY - 1, PARTS)), dma((NY - 1, PARTS)),
            dma((NY,)), dma((NY,)),
            dma((NY - 1,)), dma((NY - 1,)),
        ],
        compiler_params=pltpu.CompilerParams(
            collective_id=0, has_side_effects=True, vmem_limit_bytes=VMEM_MB * 1024 * 1024),
        cost_estimate=pl.CostEstimate(flops=4 * 2048 * 1536 * 384, bytes_accessed=12 << 20, transcendentals=256 * 384),
    )(hidden_pre, grad_out, down_weight)


def solution(mesh):
    placed = (P("gy", ("gz", "gx")), P(("gx", "gz"), "gy"), P(("gz", "gx"), "gy"))
    return jax.shard_map(
        body,
        mesh=mesh,
        in_specs=placed,
        out_specs=(P("gy", ("gz", "gx")), P(("gz", "gx"), "gy")),
        check_vma=False,
    )
```

```python
import math

import jax
import jax.numpy as jnp
from jax import lax
from jax.experimental import pallas as pl
from jax.experimental.pallas import tpu as pltpu
from jax.sharding import PartitionSpec as P

MESH = pl.DeviceIdType.MESH
coeff = math.sqrt(2.0 / math.pi)

NZ, NY, NX = 8, 4, 4
BLK = 32
TOK = 256
QTR = TOK // NY
FEAT = 1536
HID = 384
TILE = 256
NT = FEAT // TILE
PARTS = 4
PIECE = HID // PARTS
ACT_SEND, ACT_PASS = (0, 1), 4
LAG_X, LAG_HALF, LAG_MUL, LAG_ADD = 1, 2, 3, 6
LAST = 14
NAME = "ffn_backward"
Y_TYPE = jnp.float32
VMEM_MB = 60
ORDER = [(p % NX) * 2 + p // NX for p in range(8)]


def kernel(h_hbm, g_hbm, w_hbm, gh_ref, dw_hbm,
           rows_all, h_ref, h_part, w_ref, act_t, product, part, mine, from_y, kept, z_out, z_in, own, full, dw_buf,
           in_sem, dw_sem, zs, zr, xs, xr, hs, hr, cs, cr, ys, yr, ts, tr, as_, ar, aos, aor, aps, apr, fs, fr, hqs, hqr):
    gx, gy, gz = lax.axis_index("gx"), lax.axis_index("gy"), lax.axis_index("gz")
    y, zh = gy // 2, gy % 2
    x, c = gz // 2, gz % 2
    z = gx

    def at_z(v):
        return {"gx": v, "gy": gy, "gz": gz}

    def at_x(o):
        return {"gx": gx, "gy": gy, "gz": ((x + o) % NX) * 2 + c}

    def at_y(v):
        return {"gx": gx, "gy": v * 2 + zh, "gz": gz}

    twin = {"gx": gx, "gy": gy, "gz": x * 2 + (1 - c)}
    far = {"gx": gx, "gy": y * 2 + (1 - zh), "gz": gz}

    def block(j, xx, cc, start=0, size=BLK):
        return rows_all.at[pl.ds(pl.multiple_of(((j * 2 + cc) * NX + xx) * BLK + start, 16), size)]

    def remote(src, dst, send, recv, to):
        return pltpu.make_async_remote_copy(
            src_ref=src, dst_ref=dst, send_sem=send, recv_sem=recv, device_id=to, device_id_type=MESH)

    def z_copy(j, up, half):
        b = block(j, x, c, half * 16, 16)
        return remote(b, b, zs.at[up, j, half], zr.at[j, half], at_z(z + 1 if up else z - 1))

    def x_copy(j, up, half):
        b = block(j, x, c, half * 16, 16)
        return remote(b, b, xs.at[up, j, half], xr.at[up, j, half], at_x(1 if up else -1))

    def x_came(j, up, half):
        b = block(j, (x + (NX - 1 if up else 1)) % NX, c, half * 16, 16)
        return remote(b, b, xs.at[up, j, half], xr.at[up, j, half], at_x(1 if up else -1))

    def half_copy(j, up):
        b = block(j, (x + (NX - 1 if up else 1)) % NX, c, 0 if up else 16, 16)
        return remote(b, b, hs.at[up, j], hr.at[up, j], at_x(1 if up else -1))

    def half_came(j, up):
        b = block(j, (x + 2) % NX, c, 0 if up else 16, 16)
        return remote(b, b, hs.at[up, j], hr.at[up, j], at_x(1 if up else -1))

    def half_of_place(j, cc):
        return rows_all.at[pl.ds(pl.multiple_of((j * 2 + cc) * NX * BLK, NX * BLK), NX * BLK)]

    def c_copy(j):
        b = half_of_place(j, c)
        return remote(b, b, cs.at[j], cr.at[j], twin)

    def c_came(j):
        b = half_of_place(j, 1 - c)
        return remote(b, b, cs.at[j], cr.at[j], twin)

    def y_copy(j, o):
        yt = (y + o) % NY
        return remote(part.at[j, pl.ds(pl.multiple_of(yt * QTR, QTR), QTR)], from_y.at[o - 1, j],
                      ys.at[o - 1, j], yr.at[o - 1, j], at_y(yt))

    def far_copy(k):
        return remote(z_out.at[k], z_in.at[k], ts.at[k], tr.at[k], far)

    def full_copy(k):
        return remote(own.at[k], full.at[pl.ds(pl.multiple_of(y * QTR, QTR), QTR)], fs.at[k], fr.at[y], at_y(k))

    def full_came(o):
        yt = (y + o) % NY
        return remote(own.at[yt], full.at[pl.ds(pl.multiple_of(yt * QTR, QTR), QTR)], fs.at[yt], fr.at[yt], at_y(yt))

    def h_copy_to(o):
        yt = (y + o) % NY
        return remote(h_ref.at[pl.ds(pl.multiple_of(yt * QTR, QTR), QTR)], h_part.at[y], hqs.at[o - 1], hqr.at[o - 1], at_y(yt))

    def h_came(o):
        return remote(h_part.at[y], h_part.at[(y + NY - o) % NY], hqs.at[o - 1], hqr.at[o - 1], at_y((y + o) % NY))

    def act_block(g, q=None):
        rows = pl.ds(0, HID) if q is None else pl.ds(q * PIECE, PIECE)
        return act_t.at[rows, pl.ds(pl.multiple_of(g * TOK, TOK), TOK)]

    other = y * 2 + 1 - zh

    def act_far(q):
        return remote(act_block(gy, q), act_block(gy, q), as_.at[q], ar.at[q], far)

    def act_far_came(q):
        return remote(act_block(other, q), act_block(other, q), as_.at[q], ar.at[q], far)

    def act_copy(o):
        return remote(act_block(gy), act_block(gy), aos.at[o - 1], aor.at[o - 1], at_y((y + o) % NY))

    def act_came(o):
        b = act_block(((y + NY - o) % NY) * 2 + zh)
        return remote(b, b, aos.at[o - 1], aor.at[o - 1], at_y((y + o) % NY))

    def act_pass(o, q):
        return remote(act_block(other, q), act_block(other, q), aps.at[o - 1, q], apr.at[o - 1, q], at_y((y + o) % NY))

    def act_passed(o, q):
        b = act_block(((y + NY - o) % NY) * 2 + 1 - zh, q)
        return remote(b, b, aps.at[o - 1, q], apr.at[o - 1, q], at_y((y + o) % NY))

    barrier = pltpu.get_barrier_semaphore()

    def greet(to):
        pl.semaphore_signal(barrier, inc=1, device_id=to, device_id_type=MESH)

    @pl.when(z > 0)
    def _():
        greet(at_z(z - 1))

    @pl.when(z < NZ - 1)
    def _():
        greet(at_z(z + 1))

    for to in (at_x(1), at_x(-1), twin, at_y((y + 1) % NY), at_y((y + 2) % NY), at_y((y + 3) % NY), far):
        greet(to)

    g_copy = pltpu.make_async_copy(g_hbm, block(z, x, c), in_sem.at[0])
    h_copies = [pltpu.make_async_copy(h_hbm.at[pl.ds(q * BLK, BLK)], h_ref.at[pl.ds(p * BLK, BLK)], in_sem.at[2 + p])
                for p, q in enumerate(ORDER)]
    w_copy = pltpu.make_async_copy(w_hbm, w_ref, in_sem.at[1])
    g_copy.start()
    for h_copy in h_copies:
        h_copy.start()
    w_copy.start()
    g_copy.wait()
    pl.semaphore_wait(barrier, 7 + (z > 0).astype(jnp.int32) + (z < NZ - 1).astype(jnp.int32))

    def spread(j):
        x_copy(j, 1, 0).start()
        x_copy(j, 0, 1).start()
        x_copy(j, 1, 1).start()
        x_copy(j, 0, 0).start()

    for half in (0, 1):
        @pl.when(z < NZ - 1)
        def _():
            z_copy(z, 1, half).start()

        @pl.when(z > 0)
        def _():
            z_copy(z, 0, half).start()

    spread(z)

    for h_copy in h_copies:
        h_copy.wait()
    for o in (1, 2, 3):
        h_copy_to(o).start()
    h_part[y] = h_ref[pl.ds(pl.multiple_of(y * QTR, QTR), QTR), :]
    hv = h_ref[...].astype(jnp.float32)
    act = 0.5 * hv * (1.0 + jnp.tanh(coeff * (hv + 0.044715 * hv * hv * hv)))
    act_t[:, pl.ds(pl.multiple_of(gy * TOK, TOK), TOK)] = act.T.astype(jnp.bfloat16)
    for o in (1, 2, 3):
        act_copy(o).start()
    act_send = jnp.where(zh == 0, ACT_SEND[0], ACT_SEND[1])
    for q in range(PARTS):
        @pl.when(act_send + q <= 0)
        def _():
            act_far(q).start()
    w_copy.wait()

    def place(d, side):
        j = jnp.where(side == 0, z - d, z + d)
        valid = (d >= 0) & (d < NZ) & (j >= 0) & (j < NZ) & ((d > 0) | (side == 0))
        return j, valid

    def step(t, carry):
        for half in (0, 1):
            for side in (0, 1):
                j, valid = place(t, side)

                @pl.when(valid)
                def _():
                    z_copy(j, 1, half).wait_recv()

                    @pl.when((z < NZ - 1) if side == 0 else (z > 0))
                    def _():
                        z_copy(j, 1 - side, half).start()

        for side in (0, 1):
            j, valid = place(t, side)

            @pl.when(valid)
            def _():
                spread(j)

        for q in range(PARTS):
            @pl.when(t == act_send + q)
            def _():
                act_far(q).start()

        for side in (0, 1):
            j, valid = place(t - LAG_X, side)

            @pl.when(valid)
            def _():
                x_came(j, 1, 0).wait_recv()
                half_copy(j, 1).start()
                x_came(j, 0, 1).wait_recv()
                half_copy(j, 0).start()

        for side in (0, 1):
            j, valid = place(t - LAG_HALF, side)

            @pl.when(valid)
            def _():
                x_came(j, 1, 1).wait_recv()
                x_came(j, 0, 0).wait_recv()
                half_came(j, 1).wait_recv()
                half_came(j, 0).wait_recv()
                c_copy(j).start()

        def multiply(side, carry):
            j, valid = place(t - LAG_MUL, side)

            @pl.when(valid)
            def _():
                c_came(j).wait_recv()
                product[...] = lax.dot_general(
                    rows_all[pl.ds(pl.multiple_of(j * TOK, TOK), TOK), :], w_ref[...],
                    (((1,), (1,)), ((), ())), preferred_element_type=jnp.float32)
                part[j] = product[...].astype(part.dtype)
                mine[j] = product[pl.ds(pl.multiple_of(y * QTR, QTR), QTR), :]
                for o in (1, 2, 3):
                    y_copy(j, o).start()

            return carry

        lax.fori_loop(0, 2, multiply, 0)

        def add(side, carry):
            j, valid = place(t - LAG_ADD, side)

            @pl.when(valid)
            def _():
                for o in (1, 2, 3):
                    y_copy(j, o).wait_recv()
                total = mine[j]
                for o in (0, 1, 2):
                    total = total + from_y[o, j].astype(jnp.float32)
                k = j // 2

                @pl.when(j % 2 == zh)
                def _():
                    kept[k] = total

                @pl.when(j % 2 != zh)
                def _():
                    z_out[k] = total.astype(jnp.bfloat16)
                    far_copy(k).start()

            return carry

        lax.fori_loop(0, 2, add, 0)

        for q in range(PARTS):
            @pl.when(t == ACT_PASS + q)
            def _():
                act_far_came(q).wait_recv()
                for o in (1, 2, 3):
                    act_pass(o, q).start()

        return carry

    lax.fori_loop(1, LAST, step, 0)

    def dw_copy(n):
        cols = pl.ds(pl.multiple_of(n * TILE, TILE), TILE)
        return pltpu.make_async_copy(dw_buf.at[:, cols], dw_hbm.at[:, cols], dw_sem.at[n])

    def weight_tile(n, carry):
        cols = pl.ds(pl.multiple_of(n * TILE, TILE), TILE)
        dw_buf[:, cols] = jnp.dot(act_t[...], rows_all[:, cols], preferred_element_type=jnp.float32)
        dw_copy(n).start()
        return carry


    def finish(d, carry):
        for side in (0, 1):
            j, valid = place(d, side)

            @pl.when(valid & (j % 2 == zh))
            def _():
                k = j // 2
                far_copy(k).wait_recv()
                grad_act = kept[k] + z_in[k].astype(jnp.float32)
                hk = h_part[k].astype(jnp.float32)
                tk = jnp.tanh(coeff * (hk + 0.044715 * hk * hk * hk))
                slope = 0.5 * (1.0 + tk) + 0.5 * hk * (1.0 - tk * tk) * coeff * (1.0 + 3.0 * 0.044715 * hk * hk)
                result = (grad_act * slope).astype(jnp.bfloat16)

                @pl.when(k == y)
                def _():
                    full[pl.ds(pl.multiple_of(y * QTR, QTR), QTR), :] = result

                @pl.when(k != y)
                def _():
                    own[k] = result
                    full_copy(k).start()

        return carry

    for o in (1, 2, 3):
        h_came(o).wait_recv()
        act_came(o).wait_recv()

    lax.fori_loop(0, NZ, finish, 0)
    for o in (1, 2, 3):
        for q in range(PARTS):
            act_passed(o, q).wait_recv()
    lax.fori_loop(0, NT, weight_tile, 0)

    def sent(j, carry):
        for half in (0, 1):
            @pl.when((z < NZ - 1) & (j <= z))
            def _():
                z_copy(j, 1, half).wait_send()

            @pl.when((z > 0) & (j >= z))
            def _():
                z_copy(j, 0, half).wait_send()

        for up in (0, 1):
            x_copy(j, up, 0).wait_send()
            x_copy(j, up, 1).wait_send()
            half_copy(j, up).wait_send()
        c_copy(j).wait_send()
        for o in (1, 2, 3):
            y_copy(j, o).wait_send()
        return carry

    lax.fori_loop(0, NZ, sent, 0)
    for q in range(PARTS):
        act_far(q).wait_send()
    for o in (1, 2, 3):
        act_copy(o).wait_send()
        for q in range(PARTS):
            act_pass(o, q).wait_send()

    for o in (1, 2, 3):
        h_copy_to(o).wait_send()

    def sent_sums(k, carry):
        far_copy(k).wait_send()

        @pl.when(k != y)
        def _():
            full_copy(k).wait_send()

        return carry

    lax.fori_loop(0, NY, sent_sums, 0)

    for o in (1, 2, 3):
        full_came(o).wait_recv()
    for p, q in enumerate(ORDER):
        rows = slice(p * BLK, (p + 1) * BLK)
        gh_ref[q * BLK:(q + 1) * BLK, :] = full[rows, :]

    def stored(n, carry):
        dw_copy(n).wait()
        return carry

    lax.fori_loop(0, NT, stored, 0)


def body(hidden_pre, grad_out, down_weight):
    vmem = pl.BlockSpec(memory_space=pltpu.VMEM)
    hbm = pl.BlockSpec(memory_space=pl.ANY)
    dma = pltpu.SemaphoreType.DMA
    return pl.pallas_call(
        kernel,
        name=NAME,
        out_shape=(pltpu.VMEM((TOK, HID), jnp.bfloat16), pltpu.VMEM((HID, FEAT), jnp.float32)),
        in_specs=[hbm, hbm, hbm],
        out_specs=(vmem, hbm),
        scratch_shapes=[
            pltpu.VMEM((NZ * TOK, FEAT), jnp.bfloat16),
            pltpu.VMEM((TOK, HID), jnp.bfloat16),
            pltpu.VMEM((NY, QTR, HID), jnp.bfloat16),
            pltpu.VMEM((HID, FEAT), jnp.bfloat16),
            pltpu.VMEM((HID, NZ * TOK), jnp.bfloat16),
            pltpu.VMEM((TOK, HID), jnp.float32),
            pltpu.VMEM((NZ, TOK, HID), Y_TYPE),
            pltpu.VMEM((NZ, QTR, HID), jnp.float32),
            pltpu.VMEM((NY - 1, NZ, QTR, HID), Y_TYPE),
            pltpu.VMEM((NY, QTR, HID), jnp.float32),
            pltpu.VMEM((NY, QTR, HID), jnp.bfloat16),
            pltpu.VMEM((NY, QTR, HID), jnp.bfloat16),
            pltpu.VMEM((NY, QTR, HID), jnp.bfloat16),
            pltpu.VMEM((TOK, HID), jnp.bfloat16),
            pltpu.VMEM((HID, FEAT), jnp.float32),
            dma((10,)), dma((NT,)),
            dma((2, NZ, 2)), dma((NZ, 2)),
            dma((2, NZ, 2)), dma((2, NZ, 2)),
            dma((2, NZ)), dma((2, NZ)),
            dma((NZ,)), dma((NZ,)),
            dma((NY - 1, NZ)), dma((NY - 1, NZ)),
            dma((NY,)), dma((NY,)),
            dma((PARTS,)), dma((PARTS,)), dma((NY - 1,)), dma((NY - 1,)),
            dma((NY - 1, PARTS)), dma((NY - 1, PARTS)),
            dma((NY,)), dma((NY,)),
            dma((NY - 1,)), dma((NY - 1,)),
        ],
        compiler_params=pltpu.CompilerParams(
            collective_id=0, has_side_effects=True, vmem_limit_bytes=VMEM_MB * 1024 * 1024),
        cost_estimate=pl.CostEstimate(flops=4 * 2048 * 1536 * 384, bytes_accessed=12 << 20, transcendentals=256 * 384),
    )(hidden_pre, grad_out, down_weight)


def solution(mesh):
    placed = (P("gy", ("gz", "gx")), P(("gx", "gz"), "gy"), P(("gz", "gx"), "gy"))
    return jax.shard_map(
        body,
        mesh=mesh,
        in_specs=placed,
        out_specs=(P("gy", ("gz", "gx")), P(("gz", "gx"), "gy")),
        check_vma=False,
    )
```

```python
import math

import jax
import jax.numpy as jnp
from jax import lax
from jax.experimental import pallas as pl
from jax.experimental.pallas import tpu as pltpu
from jax.sharding import PartitionSpec as P

MESH = pl.DeviceIdType.MESH
coeff = math.sqrt(2.0 / math.pi)

NZ, NY, NX = 8, 4, 4
BLK = 32
TOK = 256
QTR = TOK // NY
FEAT = 1536
HID = 384
TILE = 512
NT = FEAT // TILE
PARTS = 4
PIECE = HID // PARTS
ACT_SEND, ACT_PASS = (0, 1), 4
LAG_X, LAG_HALF, LAG_MUL, LAG_ADD = 1, 2, 3, 5
LAST = 13
NAME = "ffn_backward"
Y_TYPE = jnp.bfloat16
VMEM_MB = 60
ORDER = [(p % NX) * 2 + p // NX for p in range(8)]


def kernel(h_hbm, g_hbm, w_hbm, gh_ref, dw_ref,
           rows_all, h_ref, h_part, w_ref, act_t, product, part, mine, from_y, kept, z_out, z_in, own, full,
           in_sem, zs, zr, xs, xr, hs, hr, cs, cr, ys, yr, ts, tr, as_, ar, aos, aor, aps, apr, fs, fr, hqs, hqr):
    gx, gy, gz = lax.axis_index("gx"), lax.axis_index("gy"), lax.axis_index("gz")
    y, zh = gy // 2, gy % 2
    x, c = gz // 2, gz % 2
    z = gx

    def at_z(v):
        return {"gx": v, "gy": gy, "gz": gz}

    def at_x(o):
        return {"gx": gx, "gy": gy, "gz": ((x + o) % NX) * 2 + c}

    def at_y(v):
        return {"gx": gx, "gy": v * 2 + zh, "gz": gz}

    twin = {"gx": gx, "gy": gy, "gz": x * 2 + (1 - c)}
    far = {"gx": gx, "gy": y * 2 + (1 - zh), "gz": gz}

    def block(j, xx, cc, start=0, size=BLK):
        return rows_all.at[pl.ds(pl.multiple_of(((j * 2 + cc) * NX + xx) * BLK + start, 16), size)]

    def remote(src, dst, send, recv, to):
        return pltpu.make_async_remote_copy(
            src_ref=src, dst_ref=dst, send_sem=send, recv_sem=recv, device_id=to, device_id_type=MESH)

    def z_copy(j, up, half):
        b = block(j, x, c, half * 16, 16)
        return remote(b, b, zs.at[up, j, half], zr.at[j, half], at_z(z + 1 if up else z - 1))

    def x_copy(j, up, half):
        b = block(j, x, c, half * 16, 16)
        return remote(b, b, xs.at[up, j, half], xr.at[up, j, half], at_x(1 if up else -1))

    def x_came(j, up, half):
        b = block(j, (x + (NX - 1 if up else 1)) % NX, c, half * 16, 16)
        return remote(b, b, xs.at[up, j, half], xr.at[up, j, half], at_x(1 if up else -1))

    def half_copy(j, up):
        b = block(j, (x + (NX - 1 if up else 1)) % NX, c, 0 if up else 16, 16)
        return remote(b, b, hs.at[up, j], hr.at[up, j], at_x(1 if up else -1))

    def half_came(j, up):
        b = block(j, (x + 2) % NX, c, 0 if up else 16, 16)
        return remote(b, b, hs.at[up, j], hr.at[up, j], at_x(1 if up else -1))

    def half_of_place(j, cc):
        return rows_all.at[pl.ds(pl.multiple_of((j * 2 + cc) * NX * BLK, NX * BLK), NX * BLK)]

    def c_copy(j):
        b = half_of_place(j, c)
        return remote(b, b, cs.at[j], cr.at[j], twin)

    def c_came(j):
        b = half_of_place(j, 1 - c)
        return remote(b, b, cs.at[j], cr.at[j], twin)

    def y_copy(j, o):
        yt = (y + o) % NY
        return remote(part.at[j, pl.ds(pl.multiple_of(yt * QTR, QTR), QTR)], from_y.at[o - 1, j],
                      ys.at[o - 1, j], yr.at[o - 1, j], at_y(yt))

    def far_copy(k):
        return remote(z_out.at[k], z_in.at[k], ts.at[k], tr.at[k], far)

    def full_copy(k):
        return remote(own.at[k], full.at[pl.ds(pl.multiple_of(y * QTR, QTR), QTR)], fs.at[k], fr.at[y], at_y(k))

    def full_came(o):
        yt = (y + o) % NY
        return remote(own.at[yt], full.at[pl.ds(pl.multiple_of(yt * QTR, QTR), QTR)], fs.at[yt], fr.at[yt], at_y(yt))

    def h_copy_to(o):
        yt = (y + o) % NY
        return remote(h_ref.at[pl.ds(pl.multiple_of(yt * QTR, QTR), QTR)], h_part.at[y], hqs.at[o - 1], hqr.at[o - 1], at_y(yt))

    def h_came(o):
        return remote(h_part.at[y], h_part.at[(y + NY - o) % NY], hqs.at[o - 1], hqr.at[o - 1], at_y((y + o) % NY))

    def act_block(g, q=None):
        rows = pl.ds(0, HID) if q is None else pl.ds(q * PIECE, PIECE)
        return act_t.at[rows, pl.ds(pl.multiple_of(g * TOK, TOK), TOK)]

    other = y * 2 + 1 - zh

    def act_far(q):
        return remote(act_block(gy, q), act_block(gy, q), as_.at[q], ar.at[q], far)

    def act_far_came(q):
        return remote(act_block(other, q), act_block(other, q), as_.at[q], ar.at[q], far)

    def act_copy(o):
        return remote(act_block(gy), act_block(gy), aos.at[o - 1], aor.at[o - 1], at_y((y + o) % NY))

    def act_came(o):
        b = act_block(((y + NY - o) % NY) * 2 + zh)
        return remote(b, b, aos.at[o - 1], aor.at[o - 1], at_y((y + o) % NY))

    def act_pass(o, q):
        return remote(act_block(other, q), act_block(other, q), aps.at[o - 1, q], apr.at[o - 1, q], at_y((y + o) % NY))

    def act_passed(o, q):
        b = act_block(((y + NY - o) % NY) * 2 + 1 - zh, q)
        return remote(b, b, aps.at[o - 1, q], apr.at[o - 1, q], at_y((y + o) % NY))

    barrier = pltpu.get_barrier_semaphore()

    def greet(to):
        pl.semaphore_signal(barrier, inc=1, device_id=to, device_id_type=MESH)

    @pl.when(z > 0)
    def _():
        greet(at_z(z - 1))

    @pl.when(z < NZ - 1)
    def _():
        greet(at_z(z + 1))

    for to in (at_x(1), at_x(-1), twin, at_y((y + 1) % NY), at_y((y + 2) % NY), at_y((y + 3) % NY), far):
        greet(to)

    g_copy = pltpu.make_async_copy(g_hbm, block(z, x, c), in_sem.at[0])
    h_copies = [pltpu.make_async_copy(h_hbm.at[pl.ds(q * BLK, BLK)], h_ref.at[pl.ds(p * BLK, BLK)], in_sem.at[2 + p])
                for p, q in enumerate(ORDER)]
    w_copy = pltpu.make_async_copy(w_hbm, w_ref, in_sem.at[1])
    g_copy.start()
    for h_copy in h_copies:
        h_copy.start()
    w_copy.start()
    g_copy.wait()
    pl.semaphore_wait(barrier, 7 + (z > 0).astype(jnp.int32) + (z < NZ - 1).astype(jnp.int32))

    def spread(j):
        x_copy(j, 1, 0).start()
        x_copy(j, 0, 1).start()
        x_copy(j, 1, 1).start()
        x_copy(j, 0, 0).start()

    for half in (0, 1):
        @pl.when(z < NZ - 1)
        def _():
            z_copy(z, 1, half).start()

        @pl.when(z > 0)
        def _():
            z_copy(z, 0, half).start()

    spread(z)

    for h_copy in h_copies:
        h_copy.wait()
    for o in (1, 2, 3):
        h_copy_to(o).start()
    h_part[y] = h_ref[pl.ds(pl.multiple_of(y * QTR, QTR), QTR), :]
    hv = h_ref[...].astype(jnp.float32)
    act = 0.5 * hv * (1.0 + jnp.tanh(coeff * (hv + 0.044715 * hv * hv * hv)))
    act_t[:, pl.ds(pl.multiple_of(gy * TOK, TOK), TOK)] = act.T.astype(jnp.bfloat16)
    for o in (1, 2, 3):
        act_copy(o).start()
    act_send = jnp.where(zh == 0, ACT_SEND[0], ACT_SEND[1])
    for q in range(PARTS):
        @pl.when(act_send + q <= 0)
        def _():
            act_far(q).start()
    w_copy.wait()

    def place(d, side):
        j = jnp.where(side == 0, z - d, z + d)
        valid = (d >= 0) & (d < NZ) & (j >= 0) & (j < NZ) & ((d > 0) | (side == 0))
        return j, valid

    def step(t, carry):
        for half in (0, 1):
            for side in (0, 1):
                j, valid = place(t, side)

                @pl.when(valid)
                def _():
                    z_copy(j, 1, half).wait_recv()

                    @pl.when((z < NZ - 1) if side == 0 else (z > 0))
                    def _():
                        z_copy(j, 1 - side, half).start()

        for side in (0, 1):
            j, valid = place(t, side)

            @pl.when(valid)
            def _():
                spread(j)

        for q in range(PARTS):
            @pl.when(t == act_send + q)
            def _():
                act_far(q).start()

        for side in (0, 1):
            j, valid = place(t - LAG_X, side)

            @pl.when(valid)
            def _():
                x_came(j, 1, 0).wait_recv()
                half_copy(j, 1).start()
                x_came(j, 0, 1).wait_recv()
                half_copy(j, 0).start()

        for side in (0, 1):
            j, valid = place(t - LAG_HALF, side)

            @pl.when(valid)
            def _():
                x_came(j, 1, 1).wait_recv()
                x_came(j, 0, 0).wait_recv()
                half_came(j, 1).wait_recv()
                half_came(j, 0).wait_recv()
                c_copy(j).start()

        def multiply(side, carry):
            j, valid = place(t - LAG_MUL, side)

            @pl.when(valid)
            def _():
                c_came(j).wait_recv()
                product[...] = lax.dot_general(
                    rows_all[pl.ds(pl.multiple_of(j * TOK, TOK), TOK), :], w_ref[...],
                    (((1,), (1,)), ((), ())), preferred_element_type=jnp.float32)
                part[j] = product[...].astype(part.dtype)
                mine[j] = product[pl.ds(pl.multiple_of(y * QTR, QTR), QTR), :]
                for o in (1, 2, 3):
                    y_copy(j, o).start()

            return carry

        lax.fori_loop(0, 2, multiply, 0)

        def add(side, carry):
            j, valid = place(t - LAG_ADD, side)

            @pl.when(valid)
            def _():
                for o in (1, 2, 3):
                    y_copy(j, o).wait_recv()
                total = mine[j]
                for o in (0, 1, 2):
                    total = total + from_y[o, j].astype(jnp.float32)
                k = j // 2

                @pl.when(j % 2 == zh)
                def _():
                    kept[k] = total

                @pl.when(j % 2 != zh)
                def _():
                    z_out[k] = total.astype(jnp.bfloat16)
                    far_copy(k).start()

            return carry

        lax.fori_loop(0, 2, add, 0)

        for q in range(PARTS):
            @pl.when(t == ACT_PASS + q)
            def _():
                act_far_came(q).wait_recv()
                for o in (1, 2, 3):
                    act_pass(o, q).start()

        return carry

    lax.fori_loop(1, LAST, step, 0)

    def weight_tile(n, carry):
        cols = pl.ds(pl.multiple_of(n * TILE, TILE), TILE)
        dw_ref[:, cols] = jnp.dot(act_t[...], rows_all[:, cols], preferred_element_type=jnp.float32)
        return carry


    def finish(d, carry):
        for side in (0, 1):
            j, valid = place(d, side)

            @pl.when(valid & (j % 2 == zh))
            def _():
                k = j // 2
                far_copy(k).wait_recv()
                grad_act = kept[k] + z_in[k].astype(jnp.float32)
                hk = h_part[k].astype(jnp.float32)
                tk = jnp.tanh(coeff * (hk + 0.044715 * hk * hk * hk))
                slope = 0.5 * (1.0 + tk) + 0.5 * hk * (1.0 - tk * tk) * coeff * (1.0 + 3.0 * 0.044715 * hk * hk)
                result = (grad_act * slope).astype(jnp.bfloat16)

                @pl.when(k == y)
                def _():
                    full[pl.ds(pl.multiple_of(y * QTR, QTR), QTR), :] = result

                @pl.when(k != y)
                def _():
                    own[k] = result
                    full_copy(k).start()

        return carry

    for o in (1, 2, 3):
        h_came(o).wait_recv()
        act_came(o).wait_recv()

    lax.fori_loop(0, NZ, finish, 0)
    for o in (1, 2, 3):
        for q in range(PARTS):
            act_passed(o, q).wait_recv()
    lax.fori_loop(0, NT, weight_tile, 0)

    def sent(j, carry):
        for half in (0, 1):
            @pl.when((z < NZ - 1) & (j <= z))
            def _():
                z_copy(j, 1, half).wait_send()

            @pl.when((z > 0) & (j >= z))
            def _():
                z_copy(j, 0, half).wait_send()

        for up in (0, 1):
            x_copy(j, up, 0).wait_send()
            x_copy(j, up, 1).wait_send()
            half_copy(j, up).wait_send()
        c_copy(j).wait_send()
        for o in (1, 2, 3):
            y_copy(j, o).wait_send()
        return carry

    lax.fori_loop(0, NZ, sent, 0)
    for q in range(PARTS):
        act_far(q).wait_send()
    for o in (1, 2, 3):
        act_copy(o).wait_send()
        for q in range(PARTS):
            act_pass(o, q).wait_send()

    for o in (1, 2, 3):
        h_copy_to(o).wait_send()

    def sent_sums(k, carry):
        far_copy(k).wait_send()

        @pl.when(k != y)
        def _():
            full_copy(k).wait_send()

        return carry

    lax.fori_loop(0, NY, sent_sums, 0)

    for o in (1, 2, 3):
        full_came(o).wait_recv()
    for p, q in enumerate(ORDER):
        rows = slice(p * BLK, (p + 1) * BLK)
        gh_ref[q * BLK:(q + 1) * BLK, :] = full[rows, :]


def body(hidden_pre, grad_out, down_weight):
    vmem = pl.BlockSpec(memory_space=pltpu.VMEM)
    hbm = pl.BlockSpec(memory_space=pl.ANY)
    dma = pltpu.SemaphoreType.DMA
    return pl.pallas_call(
        kernel,
        name=NAME,
        out_shape=(pltpu.VMEM((TOK, HID), jnp.bfloat16), pltpu.VMEM((HID, FEAT), jnp.float32)),
        in_specs=[hbm, hbm, hbm],
        out_specs=(vmem, vmem),
        scratch_shapes=[
            pltpu.VMEM((NZ * TOK, FEAT), jnp.bfloat16),
            pltpu.VMEM((TOK, HID), jnp.bfloat16),
            pltpu.VMEM((NY, QTR, HID), jnp.bfloat16),
            pltpu.VMEM((HID, FEAT), jnp.bfloat16),
            pltpu.VMEM((HID, NZ * TOK), jnp.bfloat16),
            pltpu.VMEM((TOK, HID), jnp.float32),
            pltpu.VMEM((NZ, TOK, HID), Y_TYPE),
            pltpu.VMEM((NZ, QTR, HID), jnp.float32),
            pltpu.VMEM((NY - 1, NZ, QTR, HID), Y_TYPE),
            pltpu.VMEM((NY, QTR, HID), jnp.float32),
            pltpu.VMEM((NY, QTR, HID), jnp.bfloat16),
            pltpu.VMEM((NY, QTR, HID), jnp.bfloat16),
            pltpu.VMEM((NY, QTR, HID), jnp.bfloat16),
            pltpu.VMEM((TOK, HID), jnp.bfloat16),
            dma((10,)),
            dma((2, NZ, 2)), dma((NZ, 2)),
            dma((2, NZ, 2)), dma((2, NZ, 2)),
            dma((2, NZ)), dma((2, NZ)),
            dma((NZ,)), dma((NZ,)),
            dma((NY - 1, NZ)), dma((NY - 1, NZ)),
            dma((NY,)), dma((NY,)),
            dma((PARTS,)), dma((PARTS,)), dma((NY - 1,)), dma((NY - 1,)),
            dma((NY - 1, PARTS)), dma((NY - 1, PARTS)),
            dma((NY,)), dma((NY,)),
            dma((NY - 1,)), dma((NY - 1,)),
        ],
        compiler_params=pltpu.CompilerParams(
            collective_id=0, has_side_effects=True, vmem_limit_bytes=VMEM_MB * 1024 * 1024),
        cost_estimate=pl.CostEstimate(flops=4 * 2048 * 1536 * 384, bytes_accessed=12 << 20, transcendentals=256 * 384),
    )(hidden_pre, grad_out, down_weight)


def solution(mesh):
    placed = (P("gy", ("gz", "gx")), P(("gx", "gz"), "gy"), P(("gz", "gx"), "gy"))
    return jax.shard_map(
        body,
        mesh=mesh,
        in_specs=placed,
        out_specs=(P("gy", ("gz", "gx")), P(("gz", "gx"), "gy")),
        check_vma=False,
    )
```
